32 devices in a mesh: dp: 4 (over x, core), seq: 8 (over z, y).
Axes of the slice: x: 2, y: 2, z: 4, core: 2. Of those that a mesh axis runs over, the one named last changes fastest.
Arguments:
- activations: bfloat16 [16384, 1280], P(('dp', 'seq')), may hold values from -6 to 6
- cotangent: bfloat16 [16384, 1280], P(('dp', 'seq')), may hold values from -6 to 6
- w_proj: bfloat16 [1280, 256], P(('dp', 'seq')), may hold values from -0.15625 to 0.15625
- forward_decay: float32 [16384, 20], P(('dp', 'seq')), may hold values from -1 to 0
- reverse_decay: float32 [16384, 20], P(('dp', 'seq')), may hold values from -1 to 0
- forward_state: bfloat16 [32, 64, 1280], P(('dp', 'seq')), may hold values from -6 to 6
- reverse_state: bfloat16 [32, 64, 1280], P(('dp', 'seq')), may hold values from -6 to 6
Outputs:
- grad_inputs: bfloat16 [16384, 1280], P(('dp', 'seq'))
- grad_weight: float32 [1280, 256], P(('dp', 'seq'))
- grad_forward_decay: float32 [16384, 20], P(('dp', 'seq'))
- grad_reverse_decay: float32 [16384, 20], P(('dp', 'seq'))
The draws below stay inside these ranges and needn't reach their ends.
All inputs are finite; a program needn't handle non-finite values.
Results may differ from the reference program's by a relative error of at most 0.0085.
Values may be sent and summed in bfloat16 or wider, within the bound.
A program may use at most 192 MiB of HBM per device.

```python
import jax
import jax.numpy as jnp
from jax import lax

HEAD_COUNT = 20
N = 64
TOK_DEV = 512
DIN = 1280
SEQUENCE_ROWS = 4096
TOKEN_TOTAL = 16384
BLOCKS = 32
N_DP = 4
N_SEQ = 8


def decay_table(key, fast_share):
    random_keys = jax.random.split(key, 7)
    fast_heads = jax.random.uniform(random_keys[0], (HEAD_COUNT,)) < fast_share
    quick_rate = jax.random.uniform(random_keys[1], (HEAD_COUNT,), minval=1.0 / 50.0, maxval=1.0 / 30.0)
    slow_rate = jax.random.uniform(random_keys[2], (HEAD_COUNT,), minval=0.8, maxval=1.6) / SEQUENCE_ROWS
    baseline_rate = jnp.where(fast_heads, quick_rate, slow_rate)
    block_multiplier = jnp.exp(jax.random.uniform(random_keys[3], (BLOCKS, HEAD_COUNT), minval=jnp.log(0.5), maxval=jnp.log(2.0)))
    block_multiplier = jnp.repeat(block_multiplier, TOK_DEV, axis=0)
    jitter_level = jax.random.uniform(random_keys[4], (TOKEN_TOTAL, HEAD_COUNT), minval=0.5, maxval=1.5)
    spike_events = jax.random.uniform(random_keys[5], (TOKEN_TOTAL, HEAD_COUNT)) < 4.0 / SEQUENCE_ROWS
    spike_penalty = jnp.log(jax.random.uniform(random_keys[6], (TOKEN_TOTAL, HEAD_COUNT), minval=0.5, maxval=0.8))
    return (-(baseline_rate[None, :] * block_multiplier * jitter_level) + jnp.where(spike_events, spike_penalty, 0.0)).astype(jnp.float32)


def draw_forward_decay(key, part):
    key = jax.random.fold_in(key, 11)
    return decay_table(key, 0.5)


def draw_reverse_decay(key, part):
    key = jax.random.fold_in(key, 12)
    return decay_table(key, 0.5)


def with_spikes(drawn, own_key, source, target, shards_of, factor):
    owner, partner = [(jnp.arange(drawn.shape[dim]) // (drawn.shape[dim] // shards_of)).reshape([-1 if axis == dim else 1 for axis in range(drawn.ndim)]) for dim in (source, target)]
    chosen = jax.random.permutation(own_key, shards_of)[partner]
    strong = (owner == chosen) | (owner == (partner + shards_of // 2) % shards_of)
    return jnp.where(strong, factor * drawn, drawn)


def levels(own_key, shape, pieces, smallest, high):
    gain, own = 1.0, jax.random.fold_in(own_key, 6)
    for position, parts in pieces:
        heights = jnp.exp(jax.random.uniform(jax.random.fold_in(own, position), (parts,), jnp.float32, smallest / len(pieces), high / len(pieces)))
        gain = gain * jnp.repeat(heights, shape[position] // parts).reshape([-1 if axis == position else 1 for axis in range(len(shape))])
    return gain


def scatter_about(rng, shape, spread, bound, cuts=(), held_as=jnp.bfloat16):
    loudness = levels(rng, shape, cuts, -0.22, 0.18) if cuts else 1.0
    values = jax.random.normal(rng, shape, jnp.float32) * spread * loudness
    return jnp.minimum(jnp.maximum(values, -bound), bound).astype(held_as)


def heavy_noise(rng, shape, scale, reach, cuts, heavy, held_as=jnp.bfloat16):
    array = scale * jax.random.normal(rng, shape, jnp.float32)
    if cuts:
        array = array * levels(rng, shape, cuts, -0.22, 0.18)
    return jnp.clip(with_spikes(array, jax.random.fold_in(rng, 3), *heavy), -reach, reach).astype(held_as)


def setup_inputs(seed: int = 0) -> dict:
    splits = jax.random.split(jax.random.key(seed), 8)
    activations = heavy_noise(splits[0], (TOKEN_TOTAL, DIN), 1.0, 6.0, ((0, 32),), (0, 1, 32, 2.75))
    cotangent = scatter_about(splits[1], (TOKEN_TOTAL, DIN), 1.0, 6.0, ((0, 32),))
    w_proj = scatter_about(splits[2], (DIN, 4 * N), DIN ** -0.5, 0.15625, ((0, 32),))
    forward_decay = draw_forward_decay(jax.random.fold_in(splits[7], 71), 0)
    reverse_decay = draw_reverse_decay(jax.random.fold_in(splits[7], 71), 0)
    forward_state = scatter_about(splits[5], (BLOCKS, N, DIN), 1.0, 6.0, ((0, 32),))
    reverse_state = scatter_about(splits[6], (BLOCKS, N, DIN), 1.0, 6.0, ((0, 32),))
    return {"activations": activations, "cotangent": cotangent, "w_proj": w_proj, "forward_decay": forward_decay, "reverse_decay": reverse_decay, "forward_state": forward_state, "reverse_state": reverse_state}


precise = lax.Precision.HIGHEST


def head_columns(values, head_size):
    return jnp.repeat(values, head_size, axis=-1)


def head_sums(values, head_count):
    return values.reshape(values.shape[:-1] + (head_count, values.shape[-1] // head_count)).sum(-1)


def intra_terms(in_rows, cot_rows, b_rows, c_rows, decays):
    length, head_count = decays.shape
    head_size = in_rows.shape[1] // head_count
    scaling = b_rows.shape[1] ** -0.5
    cumulative = jnp.cumsum(decays, axis=0)
    scores = jnp.dot(b_rows, c_rows.T, preferred_element_type=jnp.float32)
    positions = jnp.arange(length)
    upper_mask = positions[:, None] <= positions[None, :]
    exponent = cumulative.T[:, None, :] - cumulative.T[:, :, None]
    decay_mat = jnp.where(upper_mask, jnp.exp(jnp.where(upper_mask, exponent, 0.0)), 0.0)
    in_heads = in_rows.astype(jnp.float32).reshape(length, head_count, head_size)
    cot_heads = cot_rows.astype(jnp.float32).reshape(length, head_count, head_size)
    products = jnp.einsum('thp,uhp->htu', in_heads, cot_heads, precision=precise)
    weighted = scaling * scores[None] * decay_mat
    mixing = jnp.sum(decay_mat * products, axis=0)
    weighted_low = lax.optimization_barrier(weighted.astype(jnp.bfloat16)).astype(jnp.float32)
    mixing_low = mixing.astype(jnp.bfloat16)
    grad_in = jnp.einsum('htu,uhp->thp', weighted_low, cot_heads, precision=precise).reshape(length, -1)
    pair_terms = weighted * products
    increment = pair_terms.sum(2) - pair_terms.sum(1)
    grad_decay = (jnp.cumsum(increment, axis=1) - increment).T
    grad_b = scaling * jnp.dot(mixing_low, c_rows, preferred_element_type=jnp.float32)
    grad_c = scaling * jnp.dot(mixing_low.T, b_rows, preferred_element_type=jnp.float32)
    return grad_in, grad_b, grad_c, grad_decay


def cross_terms(in_rows, cot_rows, b_rows, c_rows, decays, initial, carried_low):
    head_count = decays.shape[1]
    head_size = in_rows.shape[1] // head_count
    scaling = b_rows.shape[1] ** -0.5
    cumulative = jnp.cumsum(decays, axis=0)
    block_total = cumulative[-1]
    growth = jnp.exp(head_columns(cumulative, head_size))
    shrink = jnp.exp(head_columns(block_total[None, :] - cumulative, head_size))
    b_carried = jnp.dot(b_rows, carried_low, preferred_element_type=jnp.float32)
    c_initial = jnp.dot(c_rows, initial, preferred_element_type=jnp.float32)
    grad_in = shrink * b_carried
    scaled_in = in_rows.astype(jnp.float32) * shrink
    grad_b = jnp.dot(scaled_in.astype(jnp.bfloat16), carried_low.T, preferred_element_type=jnp.float32)
    scaled_cot = cot_rows.astype(jnp.float32) * growth
    grad_c = scaling * jnp.dot(scaled_cot.astype(jnp.bfloat16), initial.T, preferred_element_type=jnp.float32)
    start_terms = scaling * head_sums(scaled_cot * c_initial, head_count)
    carry_terms = head_sums(scaled_in * b_carried, head_count)
    whole_block = jnp.exp(block_total) * head_sums(jnp.sum(carried_low.astype(jnp.float32) * initial.astype(jnp.float32), axis=0), head_count)
    grad_decay = jnp.cumsum(start_terms[::-1], axis=0)[::-1] + (jnp.cumsum(carry_terms, axis=0) - carry_terms) + whole_block[None, :]
    return grad_in, grad_b, grad_c, grad_decay


def summary(cot_rows, c_rows, decays):
    head_size = cot_rows.shape[1] // decays.shape[1]
    scaling = c_rows.shape[1] ** -0.5
    cumulative = jnp.cumsum(decays, axis=0)
    growth = jnp.exp(head_columns(cumulative, head_size))
    scaled_cot = (cot_rows.astype(jnp.float32) * growth).astype(jnp.bfloat16)
    outgoing = scaling * jnp.dot(c_rows.T, scaled_cot, preferred_element_type=jnp.float32)
    return jnp.exp(cumulative[-1]), outgoing


def direction(in_blocks, cot_blocks, b_blocks, c_blocks, decay_blocks, state_blocks, backward):
    head_size = in_blocks.shape[-1] // decay_blocks.shape[-1]

    def advance(carried, block):
        in_rows, cot_rows, b_rows, c_rows, decays, initial = block
        carried_low = carried.astype(jnp.bfloat16)
        local_part = intra_terms(in_rows, cot_rows, b_rows, c_rows, decays)
        remote_part = cross_terms(in_rows, cot_rows, b_rows, c_rows, decays, initial, carried_low)
        factor, outgoing = summary(cot_rows, c_rows, decays)
        updated = head_columns(factor, head_size)[None, :] * carried + outgoing
        return updated, tuple(near_term + far_term for near_term, far_term in zip(local_part, remote_part))

    starting = jnp.zeros(state_blocks.shape[1:], jnp.float32)
    blocks = (in_blocks, cot_blocks, b_blocks, c_blocks, decay_blocks, state_blocks)
    _, results = lax.scan(advance, starting, blocks, reverse=backward)
    return results


def reference(activations, cotangent, w_proj, forward_decay, reverse_decay, forward_state, reverse_state):
    projected = jnp.dot(activations, w_proj, preferred_element_type=jnp.float32).astype(jnp.bfloat16)

    def blocked(values):
        return values.reshape(N_DP, N_SEQ, TOK_DEV, values.shape[-1])

    def reverse_blocks(values):
        return values[:, ::-1]

    def one_sequence(inputs):
        in_seq, cot_seq, proj_seq, decay_fwd_seq, decay_rev_seq, state_fwd_seq, state_rev_seq = inputs
        forward_parts = direction(in_seq, cot_seq, proj_seq[..., :N], proj_seq[..., N:2 * N], decay_fwd_seq, state_fwd_seq, True)
        reverse_parts = direction(reverse_blocks(in_seq), reverse_blocks(cot_seq), reverse_blocks(proj_seq[..., 2 * N:3 * N]), reverse_blocks(proj_seq[..., 3 * N:]), reverse_blocks(decay_rev_seq), state_rev_seq, False)
        reverse_parts = tuple(reverse_blocks(entry) for entry in reverse_parts)
        return forward_parts, reverse_parts

    sequences = (blocked(activations), blocked(cotangent), blocked(projected), blocked(forward_decay), blocked(reverse_decay), forward_state.reshape(N_DP, N_SEQ, N, DIN), reverse_state.reshape(N_DP, N_SEQ, N, DIN))
    forward_parts, reverse_parts = lax.map(one_sequence, sequences)

    def flatten(values):
        return values.reshape(TOKEN_TOTAL, values.shape[-1])

    grad_proj = jnp.concatenate([flatten(forward_parts[1]), flatten(forward_parts[2]), flatten(reverse_parts[1]), flatten(reverse_parts[2])], axis=1).astype(jnp.bfloat16)
    projected_back = jnp.dot(grad_proj, w_proj.T, preferred_element_type=jnp.float32)
    grad_inputs = (flatten(forward_parts[0]) + flatten(reverse_parts[0]) + projected_back).astype(jnp.bfloat16)
    grad_weight = jnp.dot(activations.T, grad_proj, preferred_element_type=jnp.float32)
    return grad_inputs, grad_weight, flatten(forward_parts[3]), flatten(reverse_parts[3])
```

```python
import functools

import jax
import jax.numpy as jnp
from jax import lax
from jax.experimental import pallas as pl
from jax.experimental.pallas import tpu as pltpu
from jax.sharding import PartitionSpec as P

F32, BF16 = jnp.float32, jnp.bfloat16
MESH = pl.DeviceIdType.MESH
LOG2E = 1.4426950408889634
TILE = 128
VMEM_LIMIT = 56 * 1024 * 1024


def mm(a, b, ca=1, cb=0):
    return lax.dot_general(a, b, (((ca,), (cb,)), ((), ())), preferred_element_type=F32)


def exact_mm(ones, x):
    hi = x.astype(BF16)
    rest = x - hi.astype(F32)
    mid = rest.astype(BF16)
    low = (rest - mid.astype(F32)).astype(BF16)
    return mm(ones, hi) + mm(ones, mid) + mm(ones, low)


def sum_mm(x, ones):
    hi = x.astype(BF16)
    low = (x - hi.astype(F32)).astype(BF16)
    return mm(hi, ones) + mm(low, ones)


def greet_all(n, n_seq, me):
    barrier = pltpu.get_barrier_semaphore()

    def greet(k, _):
        to = lax.rem(me + k, n)
        pl.semaphore_signal(barrier, inc=1, device_id=(to // n_seq, lax.rem(to, n_seq)), device_id_type=MESH)
        return 0

    lax.fori_loop(1, n, greet, 0)
    pl.semaphore_wait(barrier, n - 1)


def gather_kernel(n, n_seq, w_ref, out_ref, mine, recv, whole, ssem, rsem):
    me = lax.axis_index("dp") * n_seq + lax.axis_index("seq")
    rows = w_ref.shape[0]
    greet_all(n, n_seq, me)
    part = w_ref[...].astype(F32)
    half = part.shape[1] // 2
    mine[...] = jnp.concatenate([part[:, :half], part[:, half:]], axis=0).astype(BF16)

    def copy(k, slot):
        to = lax.rem(me + k, n)
        return pltpu.make_async_remote_copy(
            src_ref=mine, dst_ref=recv.at[slot], send_sem=ssem.at[k], recv_sem=rsem.at[slot],
            device_id=(to // n_seq, lax.rem(to, n_seq)), device_id_type=MESH)

    def send(k, _):
        copy(k, me).start()
        return 0

    lax.fori_loop(1, n, send, 0)

    def place(source, block):
        block = block.astype(F32)
        at = pl.ds(pl.multiple_of(source * rows, 8), rows)
        whole[at, :half] = block[:rows]
        whole[at, half:] = block[rows:]

    place(me, mine[...])

    def take(k, _):
        source = lax.rem(me + n - k, n)
        copy(k, source).wait_recv()
        place(source, recv[source])
        return 0

    lax.fori_loop(1, n, take, 0)
    out_ref[...] = whole[...].astype(BF16)

    def sent(k, _):
        copy(k, me).wait_send()
        return 0

    lax.fori_loop(1, n, sent, 0)


def scatter_kernel(n, n_seq, parts_ref, out_ref, recv, ssem, rsem):
    me = lax.axis_index("dp") * n_seq + lax.axis_index("seq")
    rows = out_ref.shape[0]
    half = out_ref.shape[1] // 2
    greet_all(n, n_seq, me)

    def copy(k, slot):
        to = lax.rem(me + k, n)
        return pltpu.make_async_remote_copy(
            src_ref=parts_ref.at[to], dst_ref=recv.at[slot], send_sem=ssem.at[k], recv_sem=rsem.at[slot],
            device_id=(to // n_seq, lax.rem(to, n_seq)), device_id_type=MESH)

    def send(k, _):
        copy(k, me).start()
        return 0

    lax.fori_loop(1, n, send, 0)

    def take(k, total):
        source = lax.rem(me + n - k, n)
        copy(k, source).wait_recv()
        return total + recv[source].astype(F32)

    total = lax.fori_loop(1, n, take, parts_ref[me].astype(F32))
    out_ref[:, :half] = total[:rows]
    out_ref[:, half:] = total[rows:]

    def sent(k, _):
        copy(k, me).wait_send()
        return 0

    lax.fori_loop(1, n, sent, 0)


def main_kernel(n_seq, heads, split,
                act, cot, w, fdec, rdec, fstate, rstate,
                gin_out, gw_out, gfd_out, grd_out,
                bcf, bcr, rowf, rowr, pad, proj, sc, macc, gx, incf, incr, colf, colr,
                msg, recv, carried, low, gbc, starts, carries, gwf, ssem, rsem):
    my_dp, me = lax.axis_index("dp"), lax.axis_index("seq")
    length, width = act.shape
    pairs = width // TILE
    state = w.shape[1] // 4
    scaling = state ** -0.5
    tiles = length // TILE
    barrier = pltpu.get_barrier_semaphore()

    def greet(k, _):
        pl.semaphore_signal(barrier, inc=1, device_id=(my_dp, lax.rem(me + k, n_seq)), device_id_type=MESH)
        return 0

    lax.fori_loop(1, n_seq, greet, 0)

    ti = lax.broadcasted_iota(jnp.int32, (length, length), 0)
    ui = lax.broadcasted_iota(jnp.int32, (length, length), 1)
    lower = jnp.where(ui <= ti, 1.0, 0.0).astype(BF16)
    upper = jnp.where(ui >= ti, 1.0, 0.0).astype(BF16)
    for dec, ones, bc, row in ((fdec, lower, bcf, rowf), (rdec, upper, bcr, rowr)):
        pad[...] = jnp.zeros_like(pad)
        pad[:, :heads] = dec[...]
        cum = exact_mm(ones, pad[...]) * LOG2E
        across = cum.T
        for h in range(heads):
            row[h] = jnp.broadcast_to(across[h:h + 1], (8, length))
            bc[h] = jnp.broadcast_to(cum[:, h:h + 1], (length, TILE))

    proj[...] = mm(act[...], w[...]).astype(BF16)
    bf, cf = proj[:, :state], proj[:, state:2 * state]
    br, cr = proj[:, 2 * state:3 * state], proj[:, 3 * state:]
    sf = scaling * mm(bf, cf, 1, 1)
    sr = scaling * mm(br, cr, 1, 1)
    sc[...] = jnp.where(ui > ti, sf, jnp.where(ui < ti, sr, sf + sr))

    lane = lax.broadcasted_iota(jnp.int32, (length, TILE), 1)
    first = lane < TILE // 2
    cft = cf.astype(F32).T.astype(BF16)
    crt = cr.astype(F32).T.astype(BF16)
    row16 = lax.broadcasted_iota(jnp.int32, (16, TILE), 0)

    def columns(p):
        return pl.ds(pl.multiple_of(p * TILE, TILE), TILE)

    def summary(p, _):
        c = cot[:, columns(p)].astype(F32)
        for d, (bc, ct, last) in enumerate(((bcf, cft, length - 1), (bcr, crt, 0))):
            g = jnp.exp2(jnp.where(first, bc[2 * p], bc[2 * p + 1]))
            out = scaling * mm(ct, (c * g).astype(BF16))
            f = g[last:last + 1]
            hi = f.astype(BF16).astype(F32)
            tail = jnp.where(row16 == 0, hi, jnp.where(row16 == 1, f - hi, 0.0))
            msg[d, :, columns(p)] = jnp.concatenate([out, tail], axis=0).astype(BF16)
        return 0

    lax.fori_loop(0, pairs, summary, 0)
    pl.semaphore_wait(barrier, n_seq - 1)

    def copy(k, slot):
        to = lax.rem(me + k, n_seq)
        return pltpu.make_async_remote_copy(
            src_ref=msg.at[jnp.where(to > me, 1, 0)], dst_ref=recv.at[slot],
            send_sem=ssem.at[k], recv_sem=rsem.at[slot],
            device_id=(my_dp, to), device_id_type=MESH)

    def send(k, _):
        copy(k, me).start()
        return 0

    lax.fori_loop(1, n_seq, send, 0)

    macc[...] = jnp.zeros_like(macc)
    incf[...] = jnp.zeros_like(incf)
    incr[...] = jnp.zeros_like(incr)
    tt = lax.broadcasted_iota(jnp.int32, (TILE, TILE), 0)
    uu = lax.broadcasted_iota(jnp.int32, (TILE, TILE), 1)
    tile_lane = uu
    half_row = lax.broadcasted_iota(jnp.int32, (1, TILE), 1) < TILE // 2
    masks = (jnp.where(half_row, 1.0, 0.0), jnp.where(half_row, 0.0, 1.0))

    def intra(p, _):
        a = act[:, columns(p)].astype(F32)
        c32 = cot[:, columns(p)].astype(F32)
        c = cot[:, columns(p)]
        am = [(a * m).astype(BF16) for m in masks]
        cm = [(c32 * m).astype(BF16) for m in masks]
        zero8 = jnp.zeros((8, TILE), F32)
        cols = [[[zero8] * tiles for _ in range(2)] for _ in range(2)]
        for i in range(tiles):
            rows = slice(i * TILE, (i + 1) * TILE)
            total = None
            mixes = [None] * tiles
            for j in range(2):
                h = 2 * p + j
                prod = mm(am[j][rows], c, 1, 1)
                fwd_t, rev_t = bcf[h, rows], bcr[h, rows]
                wl = []
                sums = [None, None]
                for q in range(tiles):
                    cs = slice(q * TILE, (q + 1) * TILE)
                    if q > i:
                        x = rowf[h, 0:1, cs] - fwd_t
                    elif q < i:
                        x = rowr[h, 0:1, cs] - rev_t
                    else:
                        x = jnp.where(uu >= tt, rowf[h, 0:1, cs] - fwd_t, rowr[h, 0:1, cs] - rev_t)
                    decay = jnp.exp2(x)
                    pt = prod[:, cs]
                    dp = decay * pt
                    mixes[q] = dp if mixes[q] is None else mixes[q] + dp
                    s = sc[rows, cs]
                    wl.append((s * decay).astype(BF16))
                    pair = s * dp
                    if q == i:
                        todo = ((0, jnp.where(uu > tt, pair, 0.0)), (1, jnp.where(uu < tt, pair, 0.0)))
                    else:
                        todo = ((0 if q > i else 1, pair),)
                    for d, term in todo:
                        sums[d] = term if sums[d] is None else sums[d] + term
                        cols[j][d][q] = cols[j][d][q] + term.reshape(TILE // 8, 8, TILE).sum(0)
                part = mm(jnp.concatenate(wl, axis=1), cm[j])
                total = part if total is None else total + part
                for d, inc in enumerate((incf, incr)):
                    summed = jnp.sum(sums[d], axis=1, keepdims=True)
                    inc[rows, :] = jnp.where(tile_lane == h, summed, inc[rows, :])
            gx[rows, columns(p)] = total
            for q in range(tiles):
                cs = slice(q * TILE, (q + 1) * TILE)
                macc[rows, cs] += mixes[q]
        for j in range(2):
            for d, col in enumerate((colf, colr)):
                col[2 * p + j] = jnp.concatenate(cols[j][d], axis=1)
        return 0

    lax.fori_loop(0, pairs, intra, 0)

    carried[...] = jnp.zeros_like(carried)

    def join(d, source):
        copy(lax.rem(me + n_seq - source, n_seq), source).wait_recv()
        tail = recv[source, state:, :].astype(F32)
        factor = tail[0:1] + tail[1:2]
        carried[d] = factor * carried[d] + recv[source, :state, :].astype(F32)

    def from_later(k, _):
        source = n_seq - 1 - k
        pl.when(source > me)(lambda: join(0, source))
        return 0

    def from_earlier(source, _):
        pl.when(source < me)(lambda: join(1, source))
        return 0

    lax.fori_loop(0, n_seq, from_later, 0)
    lax.fori_loop(0, n_seq, from_earlier, 0)
    low[...] = carried[...].astype(BF16)
    starts[...] = jnp.zeros_like(starts)
    carries[...] = jnp.zeros_like(carries)
    gbc[...] = jnp.zeros_like(gbc)
    sel_in = lax.broadcasted_iota(jnp.int32, (TILE, TILE), 0)
    sel_out = lax.broadcasted_iota(jnp.int32, (TILE, TILE), 1)

    def cross(p, wholes):
        a = act[:, columns(p)].astype(F32)
        c = cot[:, columns(p)].astype(F32)
        select = jnp.where(sel_out == 2 * p + sel_in // (TILE // 2), 1.0, 0.0).astype(BF16)
        out = []
        extra = gx[:, columns(p)]
        for d, (bc, init, b_rows, c_rows, last) in enumerate((
                (bcf, fstate, bf, cf, length - 1), (bcr, rstate, br, cr, 0))):
            cl = jnp.where(first, bc[2 * p], bc[2 * p + 1])
            end = cl[last:last + 1]
            shrink, growth = jnp.exp2(end - cl), jnp.exp2(cl)
            car, ini = low[d, :, columns(p)], init[:, columns(p)]
            b_car = mm(b_rows, car)
            c_ini = mm(c_rows, ini)
            extra = extra + shrink * b_car
            s_in, s_cot = a * shrink, c * growth
            gbc[2 * d] += mm(s_in.astype(BF16), car, 1, 1)
            gbc[2 * d + 1] += scaling * mm(s_cot.astype(BF16), ini, 1, 1)
            starts[d] += sum_mm(scaling * s_cot * c_ini, select)
            carries[d] += sum_mm(s_in * b_car, select)
            both = jnp.sum(car.astype(F32) * ini.astype(F32), axis=0, keepdims=True) * jnp.exp2(end)
            out.append(wholes[d] + sum_mm(jnp.broadcast_to(both, (8, TILE)), select))
        gx[:, columns(p)] = extra
        return tuple(out)

    wholes = lax.fori_loop(0, pairs, cross, (jnp.zeros((8, TILE), F32),) * 2)

    mix = macc[...]
    mixf = jnp.where(ui >= ti, mix, 0.0)
    mixr = jnp.where(ui <= ti, mix, 0.0)
    gbf = gbc[0] + scaling * mm(mixf.astype(BF16), cf)
    gcf = gbc[1] + scaling * mm(mixf.T.astype(BF16), bf)
    gbr = gbc[2] + scaling * mm(mixr.astype(BF16), cr)
    gcr = gbc[3] + scaling * mm(mixr.T.astype(BF16), br)
    gproj = jnp.concatenate([gbf, gcf, gbr, gcr], axis=1).astype(BF16)
    proj[...] = gproj

    def finish(p, _):
        gp = proj[...]
        wide = pl.ds(pl.multiple_of(p * 2 * TILE, 2 * TILE), 2 * TILE)
        gin_out[:, wide] = (gx[:, wide] + mm(gp, w[wide, :], 1, 1)).astype(BF16)
        gwf[wide, :] = mm(act[:, wide], gp, 0, 0)
        return 0

    lax.fori_loop(0, width // (2 * TILE), finish, 0)
    if split:
        count, rows = gw_out.shape[0], gw_out.shape[1] // 2

        def lay(k, _):
            at = pl.ds(pl.multiple_of(k * rows, 8), rows)
            gw_out[k] = jnp.concatenate([gwf[at, :TILE], gwf[at, TILE:]], axis=0).astype(BF16)
            return 0

        lax.fori_loop(0, count, lay, 0)
    else:
        gw_out[...] = gwf[...]

    below = jnp.where(ui < ti, 1.0, 0.0).astype(BF16)
    above = jnp.where(ui > ti, 1.0, 0.0).astype(BF16)
    for d, (inc, col, strict, incl, dest) in enumerate((
            (incf, colf, below, upper, gfd_out), (incr, colr, above, lower, grd_out))):
        by_head = jnp.concatenate([col[h].sum(0, keepdims=True) for h in range(heads)], axis=0)
        pad[...] = jnp.zeros_like(pad)
        pad[:, :heads] = by_head.T
        grad = exact_mm(strict, inc[...] - pad[...] + carries[d]) + exact_mm(incl, starts[d]) + wholes[d][0:1]
        dest[...] = grad[:, :heads]

    def sent(k, _):
        copy(k, me).wait_send()
        return 0

    lax.fori_loop(1, n_seq, sent, 0)


def per_device(n_dp, n_seq, activations, cotangent, w_proj, forward_decay, reverse_decay, forward_state, reverse_state):
    n = n_dp * n_seq
    length, width = activations.shape
    rows, columns = w_proj.shape
    heads = forward_decay.shape[1]
    state = columns // 4
    split = rows % 8 == 0
    in_vmem = pl.BlockSpec(memory_space=pltpu.VMEM)
    dma = pltpu.SemaphoreType.DMA
    if split:
        weights = pl.pallas_call(
            functools.partial(gather_kernel, n, n_seq),
            out_shape=jax.ShapeDtypeStruct((rows * n, columns), BF16),
            in_specs=[in_vmem], out_specs=in_vmem,
            scratch_shapes=[
                pltpu.VMEM((2 * rows, columns // 2), BF16),
                pltpu.VMEM((n, 2 * rows, columns // 2), BF16),
                pltpu.VMEM((rows * n, columns), F32),
                dma((n,)), dma((n,)),
            ],
            compiler_params=pltpu.CompilerParams(collective_id=0, has_side_effects=True, vmem_limit_bytes=VMEM_LIMIT),
        )(w_proj)
        gw_shape = jax.ShapeDtypeStruct((n, 2 * rows, columns // 2), BF16)
    else:
        weights = lax.all_gather(w_proj, ("dp", "seq"), axis=0, tiled=True)
        gw_shape = jax.ShapeDtypeStruct((width, columns), F32)
    big = lambda *shape: pltpu.VMEM(shape, F32)
    grad_inputs, gw_parts, grad_fwd, grad_rev = pl.pallas_call(
        functools.partial(main_kernel, n_seq, heads, split),
        out_shape=(
            jax.ShapeDtypeStruct((length, width), BF16), gw_shape,
            jax.ShapeDtypeStruct((length, heads), F32), jax.ShapeDtypeStruct((length, heads), F32)),
        in_specs=[in_vmem] * 7, out_specs=(in_vmem,) * 4,
        scratch_shapes=[
            big(heads, length, TILE), big(heads, length, TILE),
            big(heads, 8, length), big(heads, 8, length), big(length, TILE),
            pltpu.VMEM((length, columns), BF16),
            big(length, length), big(length, length), big(length, width),
            big(length, TILE), big(length, TILE), big(heads, 8, length), big(heads, 8, length),
            pltpu.VMEM((2, state + 16, width), BF16),
            pltpu.VMEM((n_seq, state + 16, width), BF16),
            big(2, state, width), pltpu.VMEM((2, state, width), BF16),
            big(4, length, state), big(2, length, TILE), big(2, length, TILE),
            big(width, columns),
            dma((n_seq,)), dma((n_seq,)),
        ],
        compiler_params=pltpu.CompilerParams(collective_id=1, has_side_effects=True, vmem_limit_bytes=VMEM_LIMIT),
    )(activations, cotangent, weights, forward_decay, reverse_decay, forward_state[0], reverse_state[0])
    if split:
        grad_weight = pl.pallas_call(
            functools.partial(scatter_kernel, n, n_seq),
            out_shape=jax.ShapeDtypeStruct((rows, columns), F32),
            in_specs=[in_vmem], out_specs=in_vmem,
            scratch_shapes=[pltpu.VMEM((n, 2 * rows, columns // 2), BF16), dma((n,)), dma((n,))],
            compiler_params=pltpu.CompilerParams(collective_id=2, has_side_effects=True, vmem_limit_bytes=VMEM_LIMIT),
        )(gw_parts)
    else:
        grad_weight = lax.psum_scatter(gw_parts, ("dp", "seq"), scatter_dimension=0, tiled=True)
    return grad_inputs, grad_weight, grad_fwd, grad_rev


def solution(mesh):
    rows, cube = P(("dp", "seq"), None), P(("dp", "seq"), None, None)
    return jax.shard_map(
        functools.partial(per_device, mesh.shape["dp"], mesh.shape["seq"]),
        mesh=mesh,
        in_specs=(rows,) * 5 + (cube,) * 2,
        out_specs=(rows,) * 4,
        check_vma=False,
    )
```

```python
import functools

import jax
import jax.numpy as jnp
from jax import lax
from jax.experimental import pallas as pl
from jax.experimental.pallas import tpu as pltpu
from jax.sharding import PartitionSpec as P

F32, BF16 = jnp.float32, jnp.bfloat16
MESH = pl.DeviceIdType.MESH
LOG2E = 1.4426950408889634
TILE = 128
VMEM_LIMIT = 56 * 1024 * 1024


def mm(a, b, ca=1, cb=0):
    return lax.dot_general(a, b, (((ca,), (cb,)), ((), ())), preferred_element_type=F32)


def exact_mm(x, ones):
    hi = x.astype(BF16)
    rest = x - hi.astype(F32)
    mid = rest.astype(BF16)
    low = (rest - mid.astype(F32)).astype(BF16)
    return mm(hi, ones) + mm(mid, ones) + mm(low, ones)


def sum_mm(x, ones):
    hi = x.astype(BF16)
    low = (x - hi.astype(F32)).astype(BF16)
    return mm(hi, ones) + mm(low, ones)


def main_kernel(n_seq, heads, split,
                act, cot, w_in, fdec, rdec, fstate, rstate,
                gin_out, gw_out, gfd_out, grd_out,
                bcf, bcr, rowf, rowr, pad, proj, sc, macc, gx, incf, incr, colf, colr,
                msg, recv, carried, low, gbc, starts, carries, gwf, ssem, rsem, *more):
    my_dp, me = lax.axis_index("dp"), lax.axis_index("seq")
    length, width = act.shape
    pairs = width // TILE
    state = w_in.shape[1] // 4
    scaling = state ** -0.5
    tiles = length // TILE
    barrier = pltpu.get_barrier_semaphore()

    def greet(k, _):
        pl.semaphore_signal(barrier, inc=1, device_id=(my_dp, lax.rem(me + k, n_seq)), device_id_type=MESH)
        return 0

    lax.fori_loop(1, n_seq, greet, 0)
    if split:
        (w, wslots, w_ssem, w_rsem, parts, from_core, mid, from_x, last_parts, from_seq,
         g_ssem, g_rsem) = more
        core_row = my_dp + 1 - 2 * lax.rem(my_dp, 2)
        x_row = lax.rem(my_dp + 2, 4)
        far_row = lax.rem(core_row + 2, 4)
        for other in (core_row, x_row):
            pl.semaphore_signal(barrier, inc=1, device_id=(other, me), device_id_type=MESH)
        pl.semaphore_wait(barrier, n_seq + 1)
        w_rows = w_in.shape[0]
        part = w_in[...].astype(F32)
        own = my_dp * n_seq + me
        wslots[own] = jnp.concatenate([part[:, :TILE], part[:, TILE:]], axis=0).astype(BF16)

        def w_copy(slot, send, row, seq):
            return pltpu.make_async_remote_copy(
                src_ref=wslots.at[slot], dst_ref=wslots.at[slot], send_sem=w_ssem.at[send],
                recv_sem=w_rsem.at[slot], device_id=(row, seq), device_id_type=MESH)

        def w_first(k, _):
            w_copy(own, k, my_dp, lax.rem(me + k, n_seq)).start()
            return 0

        def w_spread(s):
            slot = my_dp * n_seq + s
            w_copy(slot, n_seq + s, x_row, me).start()
            w_copy(slot, 2 * n_seq + s, core_row, me).start()

        def w_second(k, _):
            s = lax.rem(me + n_seq - k, n_seq)
            w_copy(my_dp * n_seq + s, 0, my_dp, me).wait_recv()
            w_spread(s)
            return 0

        def w_third(k, _):
            s = lax.rem(me + n_seq - k, n_seq)
            slot = x_row * n_seq + s
            w_copy(slot, 0, x_row, me).wait_recv()
            w_copy(slot, 3 * n_seq + s, core_row, me).start()
            return 0

        def w_fourth(k, _):
            s = lax.rem(me + n_seq - k, n_seq)
            w_copy(core_row * n_seq + s, 0, core_row, me).wait_recv()
            w_copy(far_row * n_seq + s, 0, core_row, me).wait_recv()
            return 0

        def w_place(d, _):
            block = wslots[d].astype(F32)
            at = pl.ds(pl.multiple_of(d * w_rows, 8), w_rows)
            gwf[at, :TILE] = block[:w_rows]
            gwf[at, TILE:] = block[w_rows:]
            return 0

        def w_sent(k, _):
            pl.when(k > 0)(lambda: w_copy(own, k, my_dp, lax.rem(me + k, n_seq)).wait_send())
            w_copy(my_dp * n_seq + k, n_seq + k, x_row, me).wait_send()
            w_copy(my_dp * n_seq + k, 2 * n_seq + k, core_row, me).wait_send()
            w_copy(x_row * n_seq + k, 3 * n_seq + k, core_row, me).wait_send()
            return 0

        lax.fori_loop(1, n_seq, w_first, 0)
        w_spread(me)
    else:
        w = w_in
        pl.semaphore_wait(barrier, n_seq - 1)

    ti = lax.broadcasted_iota(jnp.int32, (length, length), 0)
    ui = lax.broadcasted_iota(jnp.int32, (length, length), 1)
    lower = jnp.where(ui <= ti, 1.0, 0.0).astype(BF16)
    upper = jnp.where(ui >= ti, 1.0, 0.0).astype(BF16)
    if split:
        lax.fori_loop(1, n_seq, w_second, 0)
    pad[...] = jnp.zeros_like(pad)
    for dec, ones, bc, row in ((fdec, upper, bcf, rowf), (rdec, lower, bcr, rowr)):
        pad[:heads] = dec[...]
        across = exact_mm(pad[...], ones) * LOG2E
        cum = across.T
        for h in range(heads):
            row[h] = jnp.broadcast_to(across[h:h + 1], (8, length))
            bc[h] = jnp.broadcast_to(cum[:, h:h + 1], (length, TILE))

    if split:
        lax.fori_loop(0, n_seq, w_third, 0)
        lax.fori_loop(0, n_seq, w_fourth, 0)
        lax.fori_loop(0, n_seq * 4, w_place, 0)
        w[...] = gwf[...].astype(BF16)
    proj[...] = mm(act[...], w[...]).astype(BF16)
    bf, cf = proj[:, :state], proj[:, state:2 * state]
    br, cr = proj[:, 2 * state:3 * state], proj[:, 3 * state:]
    sf = scaling * mm(bf, cf, 1, 1)
    sr = scaling * mm(br, cr, 1, 1)
    sc[...] = jnp.where(ui > ti, sf, jnp.where(ui < ti, sr, sf + sr))

    lane = lax.broadcasted_iota(jnp.int32, (length, TILE), 1)
    first = lane < TILE // 2
    cft = cf.astype(F32).T.astype(BF16)
    crt = cr.astype(F32).T.astype(BF16)
    row16 = lax.broadcasted_iota(jnp.int32, (16, TILE), 0)

    def columns(p):
        return pl.ds(pl.multiple_of(p * TILE, TILE), TILE)

    def summary(p, _):
        c = cot[:, columns(p)].astype(F32)
        for d, (bc, ct, last) in enumerate(((bcf, cft, length - 1), (bcr, crt, 0))):
            g = jnp.exp2(jnp.where(first, bc[2 * p], bc[2 * p + 1]))
            out = scaling * mm(ct, (c * g).astype(BF16))
            f = g[last:last + 1]
            hi = f.astype(BF16).astype(F32)
            tail = jnp.where(row16 == 0, hi, jnp.where(row16 == 1, f - hi, 0.0))
            msg[d, :, columns(p)] = jnp.concatenate([out, tail], axis=0).astype(BF16)
        return 0

    lax.fori_loop(0, pairs, summary, 0)

    def copy(k, slot):
        to = lax.rem(me + k, n_seq)
        return pltpu.make_async_remote_copy(
            src_ref=msg.at[jnp.where(to > me, 1, 0)], dst_ref=recv.at[slot],
            send_sem=ssem.at[k], recv_sem=rsem.at[slot],
            device_id=(my_dp, to), device_id_type=MESH)

    def send(k, _):
        copy(k, me).start()
        return 0

    lax.fori_loop(1, n_seq, send, 0)

    macc[...] = jnp.zeros_like(macc)
    incf[...] = jnp.zeros_like(incf)
    incr[...] = jnp.zeros_like(incr)
    tt = lax.broadcasted_iota(jnp.int32, (TILE, TILE), 0)
    uu = lax.broadcasted_iota(jnp.int32, (TILE, TILE), 1)
    tile_lane = uu
    half_row = lax.broadcasted_iota(jnp.int32, (1, TILE), 1) < TILE // 2
    masks = (jnp.where(half_row, 1.0, 0.0), jnp.where(half_row, 0.0, 1.0))

    def intra(p, _):
        a = act[:, columns(p)].astype(F32)
        c32 = cot[:, columns(p)].astype(F32)
        c = cot[:, columns(p)]
        am = [(a * m).astype(BF16) for m in masks]
        cm = [(c32 * m).astype(BF16) for m in masks]
        zero8 = jnp.zeros((8, TILE), F32)
        cols = [[[zero8] * tiles for _ in range(2)] for _ in range(2)]
        for i in range(tiles):
            rows = slice(i * TILE, (i + 1) * TILE)
            total = None
            mixes = [None] * tiles
            for j in range(2):
                h = 2 * p + j
                prod = mm(am[j][rows], c, 1, 1)
                fwd_t, rev_t = bcf[h, rows], bcr[h, rows]
                wl = []
                sums = [None, None]
                for q in range(tiles):
                    cs = slice(q * TILE, (q + 1) * TILE)
                    if q > i:
                        x = rowf[h, 0:1, cs] - fwd_t
                    elif q < i:
                        x = rowr[h, 0:1, cs] - rev_t
                    else:
                        x = jnp.where(uu >= tt, rowf[h, 0:1, cs] - fwd_t, rowr[h, 0:1, cs] - rev_t)
                    decay = jnp.exp2(x)
                    pt = prod[:, cs]
                    dp = decay * pt
                    mixes[q] = dp if mixes[q] is None else mixes[q] + dp
                    s = sc[rows, cs]
                    wl.append((s * decay).astype(BF16))
                    pair = s * dp
                    if q == i:
                        todo = ((0, jnp.where(uu > tt, pair, 0.0)), (1, jnp.where(uu < tt, pair, 0.0)))
                    else:
                        todo = ((0 if q > i else 1, pair),)
                    for d, term in todo:
                        sums[d] = term if sums[d] is None else sums[d] + term
                        cols[j][d][q] = cols[j][d][q] + term.reshape(TILE // 8, 8, TILE).sum(0)
                part = mm(jnp.concatenate(wl, axis=1), cm[j])
                total = part if total is None else total + part
                for d, inc in enumerate((incf, incr)):
                    summed = jnp.sum(sums[d], axis=1, keepdims=True)
                    inc[rows, :] = jnp.where(tile_lane == h, summed, inc[rows, :])
            gx[rows, columns(p)] = total
            for q in range(tiles):
                cs = slice(q * TILE, (q + 1) * TILE)
                macc[rows, cs] += mixes[q]
        for j in range(2):
            for d, col in enumerate((colf, colr)):
                col[2 * p + j] = jnp.concatenate(cols[j][d], axis=1)
        return 0

    lax.fori_loop(0, pairs, intra, 0)

    carried[...] = jnp.zeros_like(carried)

    def join(d, source):
        copy(lax.rem(me + n_seq - source, n_seq), source).wait_recv()
        tail = recv[source, state:, :].astype(F32)
        factor = tail[0:1] + tail[1:2]
        carried[d] = factor * carried[d] + recv[source, :state, :].astype(F32)

    def from_later(k, _):
        source = n_seq - 1 - k
        pl.when(source > me)(lambda: join(0, source))
        return 0

    def from_earlier(source, _):
        pl.when(source < me)(lambda: join(1, source))
        return 0

    lax.fori_loop(0, n_seq, from_later, 0)
    lax.fori_loop(0, n_seq, from_earlier, 0)
    low[...] = carried[...].astype(BF16)
    starts[...] = jnp.zeros_like(starts)
    carries[...] = jnp.zeros_like(carries)
    gbc[...] = jnp.zeros_like(gbc)
    sel_in = lax.broadcasted_iota(jnp.int32, (TILE, TILE), 0)
    sel_out = lax.broadcasted_iota(jnp.int32, (TILE, TILE), 1)

    def cross(p, wholes):
        a = act[:, columns(p)].astype(F32)
        c = cot[:, columns(p)].astype(F32)
        select = jnp.where(sel_out == 2 * p + sel_in // (TILE // 2), 1.0, 0.0).astype(BF16)
        out = []
        extra = gx[:, columns(p)]
        for d, (bc, init, b_rows, c_rows, last) in enumerate((
                (bcf, fstate, bf, cf, length - 1), (bcr, rstate, br, cr, 0))):
            cl = jnp.where(first, bc[2 * p], bc[2 * p + 1])
            end = cl[last:last + 1]
            shrink, growth = jnp.exp2(end - cl), jnp.exp2(cl)
            car, ini = low[d, :, columns(p)], init[:, columns(p)]
            b_car = mm(b_rows, car)
            c_ini = mm(c_rows, ini)
            extra = extra + shrink * b_car
            s_in, s_cot = a * shrink, c * growth
            gbc[2 * d] += mm(s_in.astype(BF16), car, 1, 1)
            gbc[2 * d + 1] += scaling * mm(s_cot.astype(BF16), ini, 1, 1)
            starts[d] += sum_mm(scaling * s_cot * c_ini, select)
            carries[d] += sum_mm(s_in * b_car, select)
            both = jnp.sum(car.astype(F32) * ini.astype(F32), axis=0, keepdims=True) * jnp.exp2(end)
            out.append(wholes[d] + sum_mm(jnp.broadcast_to(both, (8, TILE)), select))
        gx[:, columns(p)] = extra
        return tuple(out)

    wholes = lax.fori_loop(0, pairs, cross, (jnp.zeros((8, TILE), F32),) * 2)

    mix = macc[...]
    mixf = jnp.where(ui >= ti, mix, 0.0)
    mixr = jnp.where(ui <= ti, mix, 0.0)
    gbf = gbc[0] + scaling * mm(mixf.astype(BF16), cf)
    gcf = gbc[1] + scaling * mm(mixf.T.astype(BF16), bf)
    gbr = gbc[2] + scaling * mm(mixr.astype(BF16), cr)
    gcr = gbc[3] + scaling * mm(mixr.T.astype(BF16), br)
    gproj = jnp.concatenate([gbf, gcf, gbr, gcr], axis=1).astype(BF16)
    proj[...] = gproj

    def weight_part(p, _):
        wide = pl.ds(pl.multiple_of(p * 2 * TILE, 2 * TILE), 2 * TILE)
        gwf[wide, :] = mm(act[:, wide], proj[...], 0, 0)
        return 0

    def input_part(p, _):
        wide = pl.ds(pl.multiple_of(p * 2 * TILE, 2 * TILE), 2 * TILE)
        gin_out[:, wide] = (gx[:, wide] + mm(proj[...], w[wide, :], 1, 1)).astype(BF16)
        return 0

    below = jnp.where(ui < ti, 1.0, 0.0).astype(BF16)
    above = jnp.where(ui > ti, 1.0, 0.0).astype(BF16)

    def decay_part(d, inc, col, strict, incl, dest):
        pad[:heads] = jnp.concatenate([col[h].sum(0, keepdims=True) for h in range(heads)], axis=0)
        grad = exact_mm((inc[...] + carries[d]).T - pad[...], strict) + exact_mm(starts[d].T, incl)
        dest[...] = (grad + wholes[d].T[:, 0:1])[:heads]

    wides = width // (2 * TILE)
    lax.fori_loop(0, wides, weight_part, 0)
    if split:
        def lay(d, _):
            at = pl.ds(pl.multiple_of(d * w_rows, 8), w_rows)
            parts[d] = jnp.concatenate([gwf[at, :TILE], gwf[at, TILE:]], axis=0).astype(BF16)
            return 0

        lax.fori_loop(0, n_seq * 4, lay, 0)

        def row_of(r):
            return pl.ds(r * n_seq, n_seq)

        def to_core(i, row):
            return pltpu.make_async_remote_copy(
                src_ref=parts.at[row_of(row)], dst_ref=from_core.at[i], send_sem=g_ssem.at[2 * n_seq + i],
                recv_sem=g_rsem.at[2 * n_seq + i], device_id=(core_row, me), device_id_type=MESH)

        def to_x(s):
            return pltpu.make_async_remote_copy(
                src_ref=mid.at[s], dst_ref=from_x.at[s], send_sem=g_ssem.at[s],
                recv_sem=g_rsem.at[s], device_id=(x_row, me), device_id_type=MESH)

        def to_seq(s, slot):
            return pltpu.make_async_remote_copy(
                src_ref=last_parts.at[s], dst_ref=from_seq.at[slot], send_sem=g_ssem.at[n_seq + s],
                recv_sem=g_rsem.at[n_seq + slot], device_id=(my_dp, s), device_id_type=MESH)

        to_core(0, far_row).start()
        to_core(1, core_row).start()
    decay_part(0, incf, colf, above, lower, gfd_out)
    if split:
        to_core(0, far_row).wait_recv()

        def second(k, _):
            s = lax.rem(me + k, n_seq)
            mid[s] = (parts[x_row * n_seq + s].astype(F32) + from_core[0, s].astype(F32)).astype(BF16)
            to_x(s).start()
            return 0

        lax.fori_loop(1, n_seq + 1, second, 0)
    lax.fori_loop(0, wides, input_part, 0)
    if split:
        to_core(1, core_row).wait_recv()

        def third_sum(s):
            to_x(s).wait_recv()
            return parts[my_dp * n_seq + s].astype(F32) + from_core[1, s].astype(F32) + from_x[s].astype(F32)

        def third(k, _):
            s = lax.rem(me + k, n_seq)
            last_parts[s] = third_sum(s).astype(BF16)
            to_seq(s, me).start()
            return 0

        lax.fori_loop(1, n_seq, third, 0)
        own_sum = third_sum(me)
    decay_part(1, incr, colr, below, upper, grd_out)
    if split:
        def fourth(k, total):
            s = lax.rem(me + n_seq - k, n_seq)
            to_seq(s, s).wait_recv()
            return total + from_seq[s].astype(F32)

        total = lax.fori_loop(1, n_seq, fourth, own_sum)
        gw_out[:, :TILE] = total[:w_rows]
        gw_out[:, TILE:] = total[w_rows:]
        to_core(0, far_row).wait_send()
        to_core(1, core_row).wait_send()

        def all_sent(k, _):
            to_x(k).wait_send()
            pl.when(k != me)(lambda: to_seq(k, me).wait_send())
            return 0

        lax.fori_loop(0, n_seq, all_sent, 0)
        lax.fori_loop(0, n_seq, w_sent, 0)
    else:
        gw_out[...] = gwf[...]

    def sent(k, _):
        copy(k, me).wait_send()
        return 0

    lax.fori_loop(1, n_seq, sent, 0)


def per_device(n_dp, n_seq, activations, cotangent, w_proj, forward_decay, reverse_decay, forward_state, reverse_state):
    n = n_dp * n_seq
    length, width = activations.shape
    rows, columns = w_proj.shape
    heads = forward_decay.shape[1]
    state = columns // 4
    split = rows % 8 == 0 and n_dp == 4
    in_vmem = pl.BlockSpec(memory_space=pltpu.VMEM)
    dma = pltpu.SemaphoreType.DMA
    low = lambda *shape: pltpu.VMEM(shape, BF16)
    big = lambda *shape: pltpu.VMEM(shape, F32)
    if split:
        weights = w_proj
        gw_shape = jax.ShapeDtypeStruct((rows, columns), F32)
        chunks = lambda *lead: low(*lead, 2 * rows, columns // 2)
        more = [
            low(width, columns), chunks(n), dma((4 * n_seq,)), dma((n,)),
            chunks(n), chunks(2, n_seq), chunks(n_seq), chunks(n_seq), chunks(n_seq), chunks(n_seq),
            dma((2 * n_seq + 2,)), dma((2 * n_seq + 2,)),
        ]
    else:
        weights = lax.all_gather(w_proj, ("dp", "seq"), axis=0, tiled=True)
        gw_shape = jax.ShapeDtypeStruct((width, columns), F32)
        more = []
    grad_inputs, grad_weight, grad_fwd, grad_rev = pl.pallas_call(
        functools.partial(main_kernel, n_seq, heads, split),
        out_shape=(
            jax.ShapeDtypeStruct((length, width), BF16), gw_shape,
            jax.ShapeDtypeStruct((heads, length), F32), jax.ShapeDtypeStruct((heads, length), F32)),
        in_specs=[in_vmem] * 7, out_specs=(in_vmem,) * 4,
        scratch_shapes=[
            big(heads, length, TILE), big(heads, length, TILE),
            big(heads, 8, length), big(heads, 8, length), big(TILE, length),
            low(length, columns),
            big(length, length), big(length, length), big(length, width),
            big(length, TILE), big(length, TILE), big(heads, 8, length), big(heads, 8, length),
            low(2, state + 16, width), low(n_seq, state + 16, width),
            big(2, state, width), low(2, state, width),
            big(4, length, state), big(2, length, TILE), big(2, length, TILE),
            big(width, columns),
            dma((n_seq,)), dma((n_seq,)),
        ] + more,
        compiler_params=pltpu.CompilerParams(collective_id=0, has_side_effects=True, vmem_limit_bytes=VMEM_LIMIT),
    )(activations, cotangent, weights, forward_decay.T, reverse_decay.T, forward_state[0], reverse_state[0])
    if not split:
        grad_weight = lax.psum_scatter(grad_weight, ("dp", "seq"), scatter_dimension=0, tiled=True)
    return grad_inputs, grad_weight, grad_fwd.T, grad_rev.T


def solution(mesh):
    rows, cube = P(("dp", "seq"), None), P(("dp", "seq"), None, None)
    return jax.shard_map(
        functools.partial(per_device, mesh.shape["dp"], mesh.shape["seq"]),
        mesh=mesh,
        in_specs=(rows,) * 5 + (cube,) * 2,
        out_specs=(rows,) * 4,
        check_vma=False,
    )
```

```python
import functools

import jax
import jax.numpy as jnp
from jax import lax
from jax.experimental import pallas as pl
from jax.experimental.pallas import tpu as pltpu
from jax.sharding import PartitionSpec as P

F32, BF16 = jnp.float32, jnp.bfloat16
MESH = pl.DeviceIdType.MESH
LOG2E = 1.4426950408889634
TILE = 128
VMEM_LIMIT = 56 * 1024 * 1024


def mm(a, b, ca=1, cb=0):
    return lax.dot_general(a, b, (((ca,), (cb,)), ((), ())), preferred_element_type=F32)


def exact_mm(x, ones):
    hi = x.astype(BF16)
    rest = x - hi.astype(F32)
    mid = rest.astype(BF16)
    low = (rest - mid.astype(F32)).astype(BF16)
    return mm(hi, ones) + mm(mid, ones) + mm(low, ones)


def sum_mm(x, ones):
    hi = x.astype(BF16)
    low = (x - hi.astype(F32)).astype(BF16)
    return mm(hi, ones) + mm(low, ones)


def main_kernel(n_seq, heads, split,
                act, cot, w_in, fdec, rdec, fstate, rstate,
                gin_out, gw_out, gfd_out, grd_out,
                bcf, bcr, rowf, rowr, pad, proj, sc, macc, gx, incf, incr, colf, colr,
                msg, recv, tails, tails_in, spread, carried, low, gbc, starts, carries, gwf, ssem, rsem, *more):
    my_dp, me = lax.axis_index("dp"), lax.axis_index("seq")
    length, width = act.shape
    pairs = width // TILE
    state = w_in.shape[1] // 4
    scaling = state ** -0.5
    tiles = length // TILE
    barrier = pltpu.get_barrier_semaphore()

    def greet(k, _):
        pl.semaphore_signal(barrier, inc=1, device_id=(my_dp, lax.rem(me + k, n_seq)), device_id_type=MESH)
        return 0

    lax.fori_loop(1, n_seq, greet, 0)
    if split:
        (w, wslots, w_ssem, w_rsem, parts, from_core, mid, from_x, last_parts, from_seq,
         g_ssem, g_rsem) = more
        core_row = my_dp + 1 - 2 * lax.rem(my_dp, 2)
        x_row = lax.rem(my_dp + 2, 4)
        far_row = lax.rem(core_row + 2, 4)
        for other in (core_row, x_row):
            pl.semaphore_signal(barrier, inc=1, device_id=(other, me), device_id_type=MESH)
        pl.semaphore_wait(barrier, n_seq + 1)
        w_rows = w_in.shape[0]
        part = w_in[...].astype(F32)
        own = my_dp * n_seq + me
        wslots[own] = jnp.concatenate([part[:, :TILE], part[:, TILE:]], axis=0).astype(BF16)

        def w_copy(slot, send, row, seq):
            return pltpu.make_async_remote_copy(
                src_ref=wslots.at[slot], dst_ref=wslots.at[slot], send_sem=w_ssem.at[send],
                recv_sem=w_rsem.at[slot], device_id=(row, seq), device_id_type=MESH)

        def w_first(k, _):
            w_copy(own, k, my_dp, lax.rem(me + k, n_seq)).start()
            return 0

        def w_spread(s):
            slot = my_dp * n_seq + s
            w_copy(slot, n_seq + s, x_row, me).start()
            w_copy(slot, 2 * n_seq + s, core_row, me).start()

        def w_second(k, _):
            s = lax.rem(me + n_seq - k, n_seq)
            w_copy(my_dp * n_seq + s, 0, my_dp, me).wait_recv()
            w_spread(s)
            return 0

        def w_third(k, _):
            s = lax.rem(me + n_seq - k, n_seq)
            slot = x_row * n_seq + s
            w_copy(slot, 0, x_row, me).wait_recv()
            w_copy(slot, 3 * n_seq + s, core_row, me).start()
            return 0

        def w_fourth(k, _):
            s = lax.rem(me + n_seq - k, n_seq)
            w_copy(core_row * n_seq + s, 0, core_row, me).wait_recv()
            w_copy(far_row * n_seq + s, 0, core_row, me).wait_recv()
            return 0

        def w_place(d, _):
            block = wslots[d].astype(F32)
            at = pl.ds(pl.multiple_of(d * w_rows, 8), w_rows)
            gwf[at, :TILE] = block[:w_rows]
            gwf[at, TILE:] = block[w_rows:]
            return 0

        def w_sent(k, _):
            pl.when(k > 0)(lambda: w_copy(own, k, my_dp, lax.rem(me + k, n_seq)).wait_send())
            w_copy(my_dp * n_seq + k, n_seq + k, x_row, me).wait_send()
            w_copy(my_dp * n_seq + k, 2 * n_seq + k, core_row, me).wait_send()
            w_copy(x_row * n_seq + k, 3 * n_seq + k, core_row, me).wait_send()
            return 0

        lax.fori_loop(1, n_seq, w_first, 0)
        w_spread(me)
    else:
        w = w_in
        pl.semaphore_wait(barrier, n_seq - 1)

    ti = lax.broadcasted_iota(jnp.int32, (length, length), 0)
    ui = lax.broadcasted_iota(jnp.int32, (length, length), 1)
    lower = jnp.where(ui <= ti, 1.0, 0.0).astype(BF16)
    upper = jnp.where(ui >= ti, 1.0, 0.0).astype(BF16)
    if split:
        lax.fori_loop(1, n_seq, w_second, 0)
    pad[...] = jnp.zeros_like(pad)
    ends = []
    for dec, ones, bc, row, last in ((fdec, upper, bcf, rowf, length - 1), (rdec, lower, bcr, rowr, 0)):
        pad[:heads] = dec[...]
        across = exact_mm(pad[...], ones) * LOG2E
        cum = across.T
        ends.append(jnp.exp2(cum[last:last + 1]))
        for h in range(heads):
            row[h] = jnp.broadcast_to(across[h:h + 1], (8, length))
            bc[h] = jnp.broadcast_to(cum[:, h:h + 1], (length, TILE))

    if split:
        lax.fori_loop(0, n_seq, w_third, 0)
        lax.fori_loop(0, n_seq, w_fourth, 0)
        lax.fori_loop(0, n_seq * 4, w_place, 0)
        w[...] = gwf[...].astype(BF16)
    proj[...] = mm(act[...], w[...]).astype(BF16)
    bf, cf = proj[:, :state], proj[:, state:2 * state]
    br, cr = proj[:, 2 * state:3 * state], proj[:, 3 * state:]
    sf = scaling * mm(bf, cf, 1, 1)
    sr = scaling * mm(br, cr, 1, 1)
    sc[...] = jnp.where(ui > ti, sf, jnp.where(ui < ti, sr, sf + sr))

    lane = lax.broadcasted_iota(jnp.int32, (length, TILE), 1)
    first = lane < TILE // 2
    cft = cf.astype(F32).T.astype(BF16)
    crt = cr.astype(F32).T.astype(BF16)
    row16 = lax.broadcasted_iota(jnp.int32, (16, TILE), 0)
    for d in range(2):
        f = ends[d]
        hi = f.astype(BF16).astype(F32)
        tails[d] = jnp.where(row16 == 0, hi, jnp.where(row16 == 1, f - hi, 0.0)).astype(BF16)

    def columns(p):
        return pl.ds(pl.multiple_of(p * TILE, TILE), TILE)

    def summary(p, _):
        c = cot[:, columns(p)].astype(F32)
        for d, (bc, ct) in enumerate(((bcf, cft), (bcr, crt))):
            g = jnp.exp2(jnp.where(first, bc[2 * p], bc[2 * p + 1]))
            out = scaling * mm(ct, (c * g).astype(BF16))
            msg[d, :, columns(p)] = out.astype(BF16)
        return 0

    lax.fori_loop(0, pairs, summary, 0)

    def copy(k, slot):
        to = lax.rem(me + k, n_seq)
        return pltpu.make_async_remote_copy(
            src_ref=msg.at[jnp.where(to > me, 1, 0)], dst_ref=recv.at[slot],
            send_sem=ssem.at[k], recv_sem=rsem.at[slot],
            device_id=(my_dp, to), device_id_type=MESH)

    def tail_copy(k, slot):
        to = lax.rem(me + k, n_seq)
        return pltpu.make_async_remote_copy(
            src_ref=tails.at[jnp.where(to > me, 1, 0)], dst_ref=tails_in.at[slot],
            send_sem=ssem.at[n_seq + k], recv_sem=rsem.at[n_seq + slot],
            device_id=(my_dp, to), device_id_type=MESH)

    def send(k, _):
        tail_copy(k, me).start()
        copy(k, me).start()
        return 0

    lax.fori_loop(1, n_seq, send, 0)

    macc[...] = jnp.zeros_like(macc)
    incf[...] = jnp.zeros_like(incf)
    incr[...] = jnp.zeros_like(incr)
    tt = lax.broadcasted_iota(jnp.int32, (TILE, TILE), 0)
    uu = lax.broadcasted_iota(jnp.int32, (TILE, TILE), 1)
    tile_lane = uu
    half_row = lax.broadcasted_iota(jnp.int32, (1, TILE), 1) < TILE // 2
    masks = (jnp.where(half_row, 1.0, 0.0), jnp.where(half_row, 0.0, 1.0))

    def intra(p, _):
        a = act[:, columns(p)].astype(F32)
        c32 = cot[:, columns(p)].astype(F32)
        c = cot[:, columns(p)]
        am = [(a * m).astype(BF16) for m in masks]
        cm = [(c32 * m).astype(BF16) for m in masks]
        zero8 = jnp.zeros((8, TILE), F32)
        cols = [[[zero8] * tiles for _ in range(2)] for _ in range(2)]
        for i in range(tiles):
            rows = slice(i * TILE, (i + 1) * TILE)
            total = None
            mixes = [None] * tiles
            for j in range(2):
                h = 2 * p + j
                prod = mm(am[j][rows], c, 1, 1)
                fwd_t, rev_t = bcf[h, rows], bcr[h, rows]
                wl = []
                sums = [None, None]
                for q in range(tiles):
                    cs = slice(q * TILE, (q + 1) * TILE)
                    if q > i:
                        x = rowf[h, 0:1, cs] - fwd_t
                    elif q < i:
                        x = rowr[h, 0:1, cs] - rev_t
                    else:
                        x = jnp.where(uu >= tt, rowf[h, 0:1, cs] - fwd_t, rowr[h, 0:1, cs] - rev_t)
                    decay = jnp.exp2(x)
                    pt = prod[:, cs]
                    dp = decay * pt
                    mixes[q] = dp if mixes[q] is None else mixes[q] + dp
                    s = sc[rows, cs]
                    wl.append((s * decay).astype(BF16))
                    pair = s * dp
                    if q == i:
                        todo = ((0, jnp.where(uu > tt, pair, 0.0)), (1, jnp.where(uu < tt, pair, 0.0)))
                    else:
                        todo = ((0 if q > i else 1, pair),)
                    for d, term in todo:
                        sums[d] = term if sums[d] is None else sums[d] + term
                        cols[j][d][q] = cols[j][d][q] + term.reshape(TILE // 8, 8, TILE).sum(0)
                part = mm(jnp.concatenate(wl, axis=1), cm[j])
                total = part if total is None else total + part
                for d, inc in enumerate((incf, incr)):
                    summed = jnp.sum(sums[d], axis=1, keepdims=True)
                    inc[rows, :] = jnp.where(tile_lane == h, summed, inc[rows, :])
            gx[rows, columns(p)] = total
            for q in range(tiles):
                cs = slice(q * TILE, (q + 1) * TILE)
                macc[rows, cs] += mixes[q]
        for j in range(2):
            for d, col in enumerate((colf, colr)):
                col[2 * p + j] = jnp.concatenate(cols[j][d], axis=1)
        return 0

    lax.fori_loop(0, pairs, intra, 0)

    carried[...] = jnp.zeros_like(carried)
    from_head = lax.broadcasted_iota(jnp.int32, (TILE, width), 0)
    to_column = lax.broadcasted_iota(jnp.int32, (TILE, width), 1)
    spread[...] = jnp.where(to_column // (width // heads) == from_head, 1.0, 0.0).astype(BF16)

    def join(d, source):
        tail_copy(lax.rem(me + n_seq - source, n_seq), source).wait_recv()
        copy(lax.rem(me + n_seq - source, n_seq), source).wait_recv()
        tail = mm(tails_in[source], spread[...])
        carried[d] = (tail[0:1] + tail[1:2]) * carried[d] + recv[source].astype(F32)

    def from_later(k, _):
        source = n_seq - 1 - k
        pl.when(source > me)(lambda: join(0, source))
        return 0

    def from_earlier(source, _):
        pl.when(source < me)(lambda: join(1, source))
        return 0

    lax.fori_loop(0, n_seq, from_later, 0)
    lax.fori_loop(0, n_seq, from_earlier, 0)
    low[...] = carried[...].astype(BF16)
    starts[...] = jnp.zeros_like(starts)
    carries[...] = jnp.zeros_like(carries)
    gbc[...] = jnp.zeros_like(gbc)
    sel_in = lax.broadcasted_iota(jnp.int32, (2 * TILE, TILE), 0)
    sel_out = lax.broadcasted_iota(jnp.int32, (2 * TILE, TILE), 1)

    def cross(p, wholes):
        wide = pl.ds(pl.multiple_of(p * 2 * TILE, 2 * TILE), 2 * TILE)
        a = act[:, wide].astype(F32)
        c = cot[:, wide].astype(F32)
        select = jnp.where(sel_out == 4 * p + sel_in // (TILE // 2), 1.0, 0.0).astype(BF16)
        out = []
        extra = gx[:, wide]
        for d, (bc, init, b_rows, c_rows, last) in enumerate((
                (bcf, fstate, bf, cf, length - 1), (bcr, rstate, br, cr, 0))):
            cl = jnp.concatenate([jnp.where(first, bc[4 * p], bc[4 * p + 1]), jnp.where(first, bc[4 * p + 2], bc[4 * p + 3])], axis=1)
            end = cl[last:last + 1]
            shrink, growth = jnp.exp2(end - cl), jnp.exp2(cl)
            car, ini = low[d, :, wide], init[:, wide]
            b_car = mm(b_rows, car)
            c_ini = mm(c_rows, ini)
            extra = extra + shrink * b_car
            s_in, s_cot = a * shrink, c * growth
            gbc[2 * d] += mm(s_in.astype(BF16), car, 1, 1)
            gbc[2 * d + 1] += scaling * mm(s_cot.astype(BF16), ini, 1, 1)
            starts[d] += sum_mm(scaling * s_cot * c_ini, select)
            carries[d] += sum_mm(s_in * b_car, select)
            both = jnp.sum(car.astype(F32) * ini.astype(F32), axis=0, keepdims=True) * jnp.exp2(end)
            out.append(wholes[d] + sum_mm(jnp.broadcast_to(both, (8, 2 * TILE)), select))
        gx[:, wide] = extra
        return tuple(out)

    wholes = lax.fori_loop(0, pairs // 2, cross, (jnp.zeros((8, TILE), F32),) * 2)

    mix = macc[...]
    mixf = jnp.where(ui >= ti, mix, 0.0)
    mixr = jnp.where(ui <= ti, mix, 0.0)
    gbf = gbc[0] + scaling * mm(mixf.astype(BF16), cf)
    gcf = gbc[1] + scaling * mm(mixf.T.astype(BF16), bf)
    gbr = gbc[2] + scaling * mm(mixr.astype(BF16), cr)
    gcr = gbc[3] + scaling * mm(mixr.T.astype(BF16), br)
    gproj = jnp.concatenate([gbf, gcf, gbr, gcr], axis=1).astype(BF16)
    proj[...] = gproj

    def weight_part(p, _):
        wide = pl.ds(pl.multiple_of(p * 2 * TILE, 2 * TILE), 2 * TILE)
        gwf[wide, :] = mm(act[:, wide], proj[...], 0, 0)
        return 0

    def input_part(p, _):
        wide = pl.ds(pl.multiple_of(p * 2 * TILE, 2 * TILE), 2 * TILE)
        gin_out[:, wide] = (gx[:, wide] + mm(proj[...], w[wide, :], 1, 1)).astype(BF16)
        return 0

    below = jnp.where(ui < ti, 1.0, 0.0).astype(BF16)
    above = jnp.where(ui > ti, 1.0, 0.0).astype(BF16)

    def decay_part(d, inc, col, strict, incl, dest):
        pad[:heads] = jnp.concatenate([col[h].sum(0, keepdims=True) for h in range(heads)], axis=0)
        grad = exact_mm((inc[...] + carries[d]).T - pad[...], strict) + exact_mm(starts[d].T, incl)
        dest[...] = (grad + wholes[d].T[:, 0:1])[:heads]

    wides = width // (2 * TILE)
    lax.fori_loop(0, wides, weight_part, 0)
    if split:
        def lay(d, _):
            at = pl.ds(pl.multiple_of(d * w_rows, 8), w_rows)
            parts[d] = jnp.concatenate([gwf[at, :TILE], gwf[at, TILE:]], axis=0).astype(BF16)
            return 0

        lax.fori_loop(0, n_seq * 4, lay, 0)

        def row_of(r):
            return pl.ds(r * n_seq, n_seq)

        def to_core(i, row):
            return pltpu.make_async_remote_copy(
                src_ref=parts.at[row_of(row)], dst_ref=from_core.at[i], send_sem=g_ssem.at[2 * n_seq + i],
                recv_sem=g_rsem.at[2 * n_seq + i], device_id=(core_row, me), device_id_type=MESH)

        def to_x(s):
            return pltpu.make_async_remote_copy(
                src_ref=mid.at[s], dst_ref=from_x.at[s], send_sem=g_ssem.at[s],
                recv_sem=g_rsem.at[s], device_id=(x_row, me), device_id_type=MESH)

        def to_seq(s, slot):
            return pltpu.make_async_remote_copy(
                src_ref=last_parts.at[s], dst_ref=from_seq.at[slot], send_sem=g_ssem.at[n_seq + s],
                recv_sem=g_rsem.at[n_seq + slot], device_id=(my_dp, s), device_id_type=MESH)

        to_core(0, far_row).start()
        to_core(1, core_row).start()
    decay_part(0, incf, colf, above, lower, gfd_out)
    if split:
        to_core(0, far_row).wait_recv()

        def second(k, _):
            s = lax.rem(me + k, n_seq)
            mid[s] = (parts[x_row * n_seq + s].astype(F32) + from_core[0, s].astype(F32)).astype(BF16)
            to_x(s).start()
            return 0

        lax.fori_loop(1, n_seq + 1, second, 0)
    lax.fori_loop(0, wides, input_part, 0)
    if split:
        to_core(1, core_row).wait_recv()

        def third_sum(s):
            to_x(s).wait_recv()
            return parts[my_dp * n_seq + s].astype(F32) + from_core[1, s].astype(F32) + from_x[s].astype(F32)

        def third(k, _):
            s = lax.rem(me + k, n_seq)
            last_parts[s] = third_sum(s).astype(BF16)
            to_seq(s, me).start()
            return 0

        lax.fori_loop(1, n_seq, third, 0)
        own_sum = third_sum(me)
    decay_part(1, incr, colr, below, upper, grd_out)
    if split:
        def fourth(k, total):
            s = lax.rem(me + n_seq - k, n_seq)
            to_seq(s, s).wait_recv()
            return total + from_seq[s].astype(F32)

        total = lax.fori_loop(1, n_seq, fourth, own_sum)
        gw_out[:, :TILE] = total[:w_rows]
        gw_out[:, TILE:] = total[w_rows:]
        to_core(0, far_row).wait_send()
        to_core(1, core_row).wait_send()

        def all_sent(k, _):
            to_x(k).wait_send()
            pl.when(k != me)(lambda: to_seq(k, me).wait_send())
            return 0

        lax.fori_loop(0, n_seq, all_sent, 0)
        lax.fori_loop(0, n_seq, w_sent, 0)
    else:
        gw_out[...] = gwf[...]

    def sent(k, _):
        copy(k, me).wait_send()
        tail_copy(k, me).wait_send()
        return 0

    lax.fori_loop(1, n_seq, sent, 0)


def per_device(n_dp, n_seq, activations, cotangent, w_proj, forward_decay, reverse_decay, forward_state, reverse_state):
    n = n_dp * n_seq
    length, width = activations.shape
    rows, columns = w_proj.shape
    heads = forward_decay.shape[1]
    state = columns // 4
    split = rows % 8 == 0 and n_dp == 4
    in_vmem = pl.BlockSpec(memory_space=pltpu.VMEM)
    dma = pltpu.SemaphoreType.DMA
    low = lambda *shape: pltpu.VMEM(shape, BF16)
    big = lambda *shape: pltpu.VMEM(shape, F32)
    if split:
        weights = w_proj
        gw_shape = jax.ShapeDtypeStruct((rows, columns), F32)
        chunks = lambda *lead: low(*lead, 2 * rows, columns // 2)
        more = [
            low(width, columns), chunks(n), dma((4 * n_seq,)), dma((n,)),
            chunks(n), chunks(2, n_seq), chunks(n_seq), chunks(n_seq), chunks(n_seq), chunks(n_seq),
            dma((2 * n_seq + 2,)), dma((2 * n_seq + 2,)),
        ]
    else:
        weights = lax.all_gather(w_proj, ("dp", "seq"), axis=0, tiled=True)
        gw_shape = jax.ShapeDtypeStruct((width, columns), F32)
        more = []
    grad_inputs, grad_weight, grad_fwd, grad_rev = pl.pallas_call(
        functools.partial(main_kernel, n_seq, heads, split),
        out_shape=(
            jax.ShapeDtypeStruct((length, width), BF16), gw_shape,
            jax.ShapeDtypeStruct((heads, length), F32), jax.ShapeDtypeStruct((heads, length), F32)),
        in_specs=[in_vmem] * 7, out_specs=(in_vmem,) * 4,
        scratch_shapes=[
            big(heads, length, TILE), big(heads, length, TILE),
            big(heads, 8, length), big(heads, 8, length), big(TILE, length),
            low(length, columns),
            big(length, length), big(length, length), big(length, width),
            big(length, TILE), big(length, TILE), big(heads, 8, length), big(heads, 8, length),
            low(2, state, width), low(n_seq, state, width),
            low(2, 16, TILE), low(n_seq, 16, TILE), low(TILE, width),
            big(2, state, width), low(2, state, width),
            big(4, length, state), big(2, length, TILE), big(2, length, TILE),
            big(width, columns),
            dma((2 * n_seq,)), dma((2 * n_seq,)),
        ] + more,
        compiler_params=pltpu.CompilerParams(collective_id=0, has_side_effects=True, vmem_limit_bytes=VMEM_LIMIT),
    )(activations, cotangent, weights, forward_decay.T, reverse_decay.T, forward_state[0], reverse_state[0])
    if not split:
        grad_weight = lax.psum_scatter(grad_weight, ("dp", "seq"), scatter_dimension=0, tiled=True)
    return grad_inputs, grad_weight, grad_fwd.T, grad_rev.T


def solution(mesh):
    rows, cube = P(("dp", "seq"), None), P(("dp", "seq"), None, None)
    return jax.shard_map(
        functools.partial(per_device, mesh.shape["dp"], mesh.shape["seq"]),
        mesh=mesh,
        in_specs=(rows,) * 5 + (cube,) * 2,
        out_specs=(rows,) * 4,
        check_vma=False,
    )
```
